32 devices in a mesh: section: 2 (over x), expert: 4 (over z), tensor: 4 (over y, core).
Axes of the slice: x: 2, y: 2, z: 4, core: 2. Of those that a mesh axis runs over, the one named last changes fastest.
Arguments:
- tokens: bfloat16 [64, 6144], P(('section', 'expert'), 'tensor'), may hold values from -6 to 6
- routes: int32 [64, 2], P(('section', 'expert')), may hold values from 0 to 3, all different within a row; in each aligned block of 8 rows (0 to 7, 8 to 15, ...) at most 8 rows name the same one
- router: float32 [6144, 4], replicated, may hold values from -0.18 to 0.18
- gate_proj: bfloat16 [4, 6144, 8192], P('expert', None, ('section', 'tensor')), may hold values from -0.078125 to 0.078125
- up_proj: bfloat16 [4, 6144, 8192], P('expert', None, ('section', 'tensor')), may hold values from -0.078125 to 0.078125
- down_proj: bfloat16 [4, 8192, 6144], P('expert', ('section', 'tensor')), may hold values from -0.09375 to 0.09375
- grad_out: bfloat16 [64, 6144], P(('section', 'expert'), 'tensor'), may hold values from -6 to 6
Outputs:
- moe_out: bfloat16 [64, 6144], P(('section', 'expert'), 'tensor')
- grad_tokens: bfloat16 [64, 6144], P(('section', 'expert'), 'tensor')
- grad_router: float32 [6144, 4], P('tensor')
The draws below stay inside these ranges and needn't reach their ends.
Inputs may be any that keep to these rules, and one draw needn't show every extreme that they name: `routes`: each token names 2 different experts; in each aligned block of 8 tokens (the tokens of one group) no expert is named by more than 8 tokens, and in some blocks one expert is named by exactly 8.
All inputs are finite; a program needn't handle non-finite values.
Results may differ from the reference program's by a relative error of at most 0.02.
Values may be sent and summed in bfloat16 or wider, within the bound.
A program may use at most 128 MiB of HBM per device.

```python
import math
import jax
import jax.numpy as jnp
import numpy as np
from jax import lax

D = 6144
FF = 8192
TOP = 2
TOK_DEV = 8
EXPERTS = 4
TOKENS = 64
CAP = 8
FF_DEV = 1024
N_SECTION = 2
N_TENSOR = 4


def strengthened(result, rng, source, target, shards_of, factor):
    owner, partner = [(jnp.arange(result.shape[dim]) // (result.shape[dim] // shards_of)).reshape([-1 if axis == dim else 1 for axis in range(result.ndim)]) for dim in (source, target)]
    chosen = jax.random.permutation(rng, shards_of)[partner]
    strong = (owner == chosen) | (owner == (partner + shards_of // 2) % shards_of)
    return jnp.where(strong, factor * result, result)


def steps_of(own_key, extent, cuts, least, high):
    loudness, own = 1.0, jax.random.fold_in(own_key, 6)
    for axis_at, shards_of in cuts:
        draws = jnp.exp(jax.random.uniform(jax.random.fold_in(own, axis_at), (shards_of,), jnp.float32, least / len(cuts), high / len(cuts)))
        loudness = loudness * jnp.repeat(draws, extent[axis_at] // shards_of).reshape([-1 if axis == axis_at else 1 for axis in range(len(extent))])
    return loudness


def shared_out(rng, own, number, rows, amount, top, limit, lean):
    ranking = jax.random.permutation(rng, amount)
    heavy_load, ordinary = shares(amount, rows * top, limit, lean, True), shares(amount, rows * top, limit, lean, False)
    places = jnp.arange(amount)

    def named(sizes, rotation):
        used = int((sizes > 0).sum())
        fixed = max(1, used // 4)
        moved = fixed + (places - fixed + rotation * (used - fixed)) % max(1, amount - fixed)
        return jnp.zeros((amount,), jnp.int32).at[ranking[jnp.where(places < fixed, places, moved)]].set(jnp.asarray(sizes, jnp.int32))

    sizes = jnp.where(number % 4 == 0, named(heavy_load, number // 4), named(ordinary, number - number // 4 - 1))
    mixed = jax.random.permutation(jax.random.fold_in(own, 3), amount)
    giver, sink = mixed[0:amount // 2 * 2:2], mixed[1:amount // 2 * 2:2]
    room = jnp.minimum(sizes[giver] - 1, limit - sizes[sink]) // 2
    room = jnp.where((giver == ranking[0]) | (sink == ranking[0]) | (sizes[sink] == 0), 0, jnp.maximum(room, 0))
    moved = jax.random.randint(jax.random.fold_in(own, 4), (amount // 2,), 0, 1 << 20) % (room + 1)
    sizes = sizes.at[giver].add(-moved).at[sink].add(moved)
    items = jnp.searchsorted(jnp.cumsum(sizes), jnp.arange(rows * top), side="right").astype(jnp.int32)
    listing = items.reshape(top, rows).T
    listing = listing[jax.random.permutation(jax.random.fold_in(own, 1), rows)]
    rotation = jax.random.randint(jax.random.fold_in(own, 2), (rows, 1), 0, top)
    return jnp.take_along_axis(listing, (jnp.arange(top)[None, :] + rotation) % top, axis=1)


def shares(count, total, limit, skew, full):
    loads = [(1 << 20) // math.isqrt(standing ** skew) + 1 for standing in range(1, count + 1)]
    largest = limit if full else min(limit, max(-(-total // count), total * loads[0] // sum(loads)))
    least = 1 if total - largest >= count - 1 else 0
    given, surplus = [largest] + [least] * (count - 1), total - largest - least * (count - 1)
    while surplus > 0:
        movable = [i for i in range(1, count) if given[i] < largest] or [i for i in range(1, count) if given[i] < limit]
        pool, budget = sum([loads[i] for i in movable]), surplus
        for i in movable:
            addition = min(limit - given[i], max(1, budget * loads[i] // pool), surplus)
            given[i] = given[i] + addition
            surplus = surplus - addition
    return np.array(given)


def centred(key, dims, scale, limit, shards=(), kind=jnp.bfloat16):
    level = steps_of(key, dims, shards, -0.22, 0.18) if shards else 1.0
    array = jax.random.normal(key, dims, jnp.float32) * scale * level
    return jnp.minimum(jnp.maximum(array, -limit), limit).astype(kind)


def heavy_noise(stream_key, extent, deviation, most, shards, heavy, kind=jnp.bfloat16):
    array = deviation * jax.random.normal(stream_key, extent, jnp.float32)
    if shards:
        array = array * steps_of(stream_key, extent, shards, -0.22, 0.18)
    return jnp.clip(strengthened(array, jax.random.fold_in(stream_key, 3), *heavy), -most, most).astype(kind)


def setup_inputs(seed: int = 0) -> dict:
    seeds = jax.random.split(jax.random.key(seed), 8)
    tokens = centred(seeds[0], (TOKENS, D), 1.0, 6.0, ((0, 8), (1, 4)))
    routes_keys = jax.random.split(jax.random.fold_in(seeds[1], 1), TOKENS // TOK_DEV)
    routes_turns = jax.random.permutation(jax.random.fold_in(seeds[1], 3), TOKENS // TOK_DEV)
    routes = jax.vmap(lambda own, number: shared_out(jax.random.fold_in(seeds[1], 2), own, number, TOK_DEV, EXPERTS, TOP, CAP, 2))(routes_keys, routes_turns).reshape((TOKENS, TOP))
    router = centred(seeds[2], (D, EXPERTS), 0.03, 0.18, (), jnp.float32)
    gate_proj = centred(seeds[3], (EXPERTS, D, FF), D ** -0.5, 0.078125, ((0, 4), (2, 8)))
    up_proj = centred(seeds[4], (EXPERTS, D, FF), D ** -0.5, 0.078125, ((0, 4), (2, 8)))
    down_proj = heavy_noise(seeds[5], (EXPERTS, FF, D), FF ** -0.5, 0.09375, ((0, 4), (1, 8)), (1, 2, 8, 2.0))
    grad_out = centred(seeds[6], (TOKENS, D), 1.0, 6.0, ((0, 8), (1, 4)))
    return dict(tokens=tokens, routes=routes, router=router, gate_proj=gate_proj, up_proj=up_proj, down_proj=down_proj, grad_out=grad_out)


precise = lax.Precision.HIGHEST


def route_table(routes, expert_count, capacity):
    flat_ids = routes.reshape(-1)
    expert_hot = (flat_ids[:, None] == jnp.arange(expert_count, dtype=jnp.int32)[None, :]).astype(jnp.float32)
    earlier = jnp.cumsum(expert_hot, axis=0) - expert_hot
    slot_ids = jnp.sum(earlier * expert_hot, axis=1).astype(jnp.int32)
    slot_hot = (slot_ids[:, None] == jnp.arange(capacity, dtype=jnp.int32)[None, :]).astype(jnp.float32)
    routing = expert_hot.T[:, None, :] * slot_hot.T[None, :, :]
    return routing.reshape(expert_count * capacity, flat_ids.shape[0])


def gate_weights(logits, routes):
    chosen = jnp.take_along_axis(logits, routes, axis=1)
    scores = jax.nn.sigmoid(chosen)
    totals = jnp.sum(scores, axis=1, keepdims=True)
    return scores, scores / totals


def expert_front(rows_x, gate_mat, up_mat):
    pre_gate = jnp.dot(rows_x, gate_mat, preferred_element_type=jnp.float32)
    pre_up = jnp.dot(rows_x, up_mat, preferred_element_type=jnp.float32)
    gate_sig = jax.nn.sigmoid(pre_gate)
    gate_act = pre_gate * gate_sig
    hidden = (gate_act * pre_up).astype(jnp.bfloat16)
    return pre_gate, pre_up, gate_sig, gate_act, hidden


def expert_grads(grad_hidden, pre_gate, pre_up, gate_sig, gate_act):
    grad_gate = (grad_hidden * pre_up * gate_sig * (1.0 + pre_gate * (1.0 - gate_sig))).astype(jnp.bfloat16)
    grad_up = (grad_hidden * gate_act).astype(jnp.bfloat16)
    return grad_gate, grad_up


def router_grads(grad_weight, scores, routes, expert_count):
    totals = scores[:, 0] + scores[:, 1]
    first = (grad_weight[:, 0] - grad_weight[:, 1]) * scores[:, 1] / (totals * totals)
    second = (grad_weight[:, 1] - grad_weight[:, 0]) * scores[:, 0] / (totals * totals)
    grad_scores = jnp.stack([first, second], axis=1)
    grad_chosen = grad_scores * scores * (1.0 - scores)
    expert_hot = (routes[:, :, None] == jnp.arange(expert_count, dtype=jnp.int32)[None, None, :]).astype(jnp.float32)
    return jnp.sum(expert_hot * grad_chosen[:, :, None], axis=1)


def rounded_term(value):
    narrow = lax.optimization_barrier(value.astype(jnp.bfloat16))
    return narrow.astype(jnp.float32)


def reference(tokens, routes, router, gate_proj, up_proj, down_proj, grad_out):
    groups = TOKENS // TOK_DEV
    shard_count = N_SECTION * N_TENSOR
    wide_tokens = tokens.astype(jnp.float32)
    logits = jnp.dot(wide_tokens, router, precision=precise)
    scores, weight = gate_weights(logits, routes)
    routing = jax.vmap(lambda part_ids: route_table(part_ids, EXPERTS, CAP))(routes.reshape(groups, TOK_DEV, TOP))
    tokens_rep = jnp.repeat(wide_tokens.reshape(groups, TOK_DEV, D), TOP, axis=1)
    grads_rep = jnp.repeat(grad_out.astype(jnp.float32).reshape(groups, TOK_DEV, D), TOP, axis=1) * weight.reshape(groups, TOK_DEV * TOP, 1)
    x_sent = jnp.einsum("gkr,grd->gkd", routing, tokens_rep, precision=precise).astype(jnp.bfloat16)
    dy_sent = jnp.einsum("gkr,grd->gkd", routing, grads_rep, precision=precise).astype(jnp.bfloat16)

    def by_expert(buffer):
        return buffer.reshape(groups, EXPERTS, CAP, D).transpose(1, 0, 2, 3).reshape(EXPERTS, groups * CAP, D)

    def split_columns(matrix):
        return matrix.reshape(matrix.shape[0], shard_count, FF_DEV).transpose(1, 0, 2)

    def expert_pass(members):
        rows_x, rows_dy, gate_mat, up_mat, down_mat = members
        pre_gate, pre_up, gate_sig, gate_act, hidden = expert_front(rows_x, gate_mat, up_mat)
        grad_hidden = jnp.dot(rows_dy, down_mat.T, preferred_element_type=jnp.float32)
        grad_gate, grad_up = expert_grads(grad_hidden, pre_gate, pre_up, gate_sig, gate_act)
        pieces = (split_columns(hidden), split_columns(grad_gate), split_columns(grad_up),
                  split_columns(gate_mat), split_columns(up_mat), down_mat.reshape(shard_count, FF_DEV, D))

        def add_block(carry, piece):
            hid_part, gg_part, gu_part, gate_part, up_part, down_part = piece
            out_term = jnp.dot(hid_part, down_part, preferred_element_type=jnp.float32)
            grad_term = jnp.dot(gg_part, gate_part.T, preferred_element_type=jnp.float32) + jnp.dot(gu_part, up_part.T, preferred_element_type=jnp.float32)
            return (carry[0] + rounded_term(out_term), carry[1] + rounded_term(grad_term)), None

        start = (jnp.zeros((rows_x.shape[0], D), jnp.float32), jnp.zeros((rows_x.shape[0], D), jnp.float32))
        (expert_out, expert_grad), _ = lax.scan(add_block, start, pieces)
        return expert_out, expert_grad

    outs_all, grads_all = lax.map(expert_pass, (by_expert(x_sent), by_expert(dy_sent), gate_proj, up_proj, down_proj))

    def to_groups(values):
        return values.reshape(EXPERTS, groups, CAP, D).transpose(1, 0, 2, 3).reshape(groups, EXPERTS * CAP, D)

    out_route = jnp.einsum("gkr,gkd->grd", routing, to_groups(outs_all), precision=precise).reshape(TOKENS, TOP, D)
    grad_route = jnp.einsum("gkr,gkd->grd", routing, to_groups(grads_all), precision=precise).reshape(TOKENS, TOP, D)
    moe_out = jnp.sum(weight[:, :, None] * out_route, axis=1).astype(jnp.bfloat16)
    grad_weight = jnp.sum(grad_out.astype(jnp.float32)[:, None, :] * out_route, axis=2)
    grad_logits = router_grads(grad_weight, scores, routes, EXPERTS)
    grad_tokens = (jnp.sum(grad_route, axis=1) + jnp.dot(grad_logits, router.T, precision=precise)).astype(jnp.bfloat16)
    grad_router = jnp.dot(wide_tokens.T, grad_logits, precision=precise)
    return moe_out, grad_tokens, grad_router
```

```python
import functools

import jax
import jax.numpy as jnp
from jax import lax
from jax.experimental import pallas as pl
from jax.experimental.pallas import tpu as pltpu
from jax.sharding import PartitionSpec as P

F32 = jnp.float32
BF16 = jnp.bfloat16
LANES = 128
precise = lax.Precision.HIGHEST


def contract_last(left, right):
    return lax.dot_general(left, right, (((1,), (1,)), ((), ())), preferred_element_type=F32)


def step_of(size, most):
    step = most
    while size % step:
        step //= 2
    return step


def layer_kernel(
    sizes,
    tokens_ref,
    routes_ref,
    router_ref,
    grad_out_ref,
    gate_hbm,
    up_hbm,
    down_hbm,
    moe_ref,
    grad_tokens_ref,
    grad_router_ref,
    gate,
    up,
    down,
    gathered,
    xs,
    dys,
    router_parts,
    router_pad,
    logits,
    acc_gate,
    acc_up,
    acc_down,
    hidden,
    grad_gate,
    grad_up,
    weight_own,
    from_sibling,
    from_plane,
    plane_sum,
    from_expert,
    gw_own,
    gw_plane,
    gw_expert,
    grad_logits,
    weight_sems,
    send_sems,
    recv_sems,
):
    sections, experts, tensors, quarter, ff_dev = sizes
    half = tensors // 2
    plane = sections * half
    groups = sections * experts
    count = groups * 8
    section = lax.axis_index("section")
    expert = lax.axis_index("expert")
    tensor = lax.axis_index("tensor")
    row = tensor // 2
    core = tensor % 2
    group = section * experts + expert
    here = {"section": section, "expert": expert, "tensor": tensor}

    def at(**moved):
        return {**here, **moved}

    def expert_peer(k):
        return at(expert=(expert + k) % experts)

    def plane_peer(k):
        return at(
            section=(section + k // half) % sections,
            tensor=((row + k % half) % half) * 2 + core,
        )

    sibling = at(tensor=row * 2 + 1 - core)
    used = [0]
    sends = []

    def remote(src, dst, peer):
        index = used[0]
        used[0] += 1
        copy = pltpu.make_async_remote_copy(
            src_ref=src,
            dst_ref=dst,
            send_sem=send_sems.at[index],
            recv_sem=recv_sems.at[index],
            device_id=peer,
            device_id_type=pl.DeviceIdType.MESH,
        )
        copy.start()
        sends.append(copy)
        return copy

    barrier = pltpu.get_barrier_semaphore()
    peers = (
        [expert_peer(k) for k in range(1, experts)]
        + [plane_peer(k) for k in range(1, plane)]
        + [sibling]
    )
    for peer in peers:
        pl.semaphore_signal(barrier, inc=1, device_id=peer, device_id_type=pl.DeviceIdType.MESH)

    def quarter_at(dy, other):
        return ((row + half - dy) % half) * 2 + (1 - core if other else core)

    order = [quarter_at(dy, other) for dy in range(half) for other in (False, True)]
    weight_copies = []
    for j, q in enumerate(order):
        span = pl.ds(pl.multiple_of(q * quarter, LANES), quarter)
        trio = [
            pltpu.make_async_copy(gate_hbm.at[span, :], gate.at[span, :], weight_sems.at[j, 0]),
            pltpu.make_async_copy(up_hbm.at[span, :], up.at[span, :], weight_sems.at[j, 1]),
            pltpu.make_async_copy(down_hbm.at[:, span], down.at[:, span], weight_sems.at[j, 2]),
        ]
        for copy in trio:
            copy.start()
        weight_copies.append(trio)

    lane8 = lax.broadcasted_iota(jnp.int32, (8, LANES), 1)
    routes = routes_ref[...]
    hot = jnp.zeros((8, LANES), F32)
    for k in range(routes.shape[1]):
        hot = jnp.where(routes[:, k : k + 1] == lane8, 1.0, hot)
    unit_rows = pl.ds(pl.multiple_of(group * 16, 16), 16)
    gathered[tensor, unit_rows, 0:quarter] = jnp.concatenate(
        [tokens_ref[...].astype(F32), grad_out_ref[...].astype(F32)], axis=0
    ).astype(BF16)
    gathered[tensor, unit_rows, quarter : quarter + LANES] = jnp.concatenate(
        [hot, jnp.zeros((8, LANES), F32)], axis=0
    ).astype(BF16)

    pl.semaphore_wait(barrier, len(peers))

    unit = gathered.at[tensor, unit_rows, :]
    over_expert = [remote(unit, unit, expert_peer(k)) for k in range(1, experts)]

    router_pad[...] = jnp.zeros_like(router_pad)
    router_pad[0:experts, :] = router_ref[...]
    wide = router_pad[...]
    high = wide.astype(BF16).astype(F32)
    middle = (wide - high).astype(BF16).astype(F32)
    low = wide - high - middle
    router_parts[...] = jnp.zeros_like(router_parts)
    router_parts[0:32, :] = jnp.concatenate(
        [high, middle, low, jnp.zeros_like(low)], axis=0
    ).astype(BF16)
    logits[...] = jnp.zeros_like(logits)
    acc_gate[...] = jnp.zeros_like(acc_gate)
    acc_up[...] = jnp.zeros_like(acc_up)
    acc_down[...] = jnp.zeros_like(acc_down)
    gw_own[...] = jnp.zeros_like(gw_own)

    for copy in over_expert:
        copy.wait_recv()

    def chunk_of(k):
        from_section = (section + sections - k // half) % sections
        from_tensor = quarter_at(k % half, False)
        rows = pl.ds(pl.multiple_of(from_section * experts * 16, 16), experts * 16)
        return gathered.at[from_tensor, rows, :]

    own_chunk = chunk_of(0)
    over_plane = {k: remote(own_chunk, own_chunk, plane_peer(k)) for k in range(1, plane)}
    over_core = {0: remote(own_chunk, own_chunk, sibling)}
    by_row = sorted(range(1, plane), key=lambda k: (k % half, k // half))
    for k in by_row:
        over_plane[k].wait_recv()
        over_core[k] = remote(chunk_of(k), chunk_of(k), sibling)

    gather_sends = len(sends)
    tile = step_of(ff_dev, 256)
    for j, q in enumerate(order):
        dy = j // 2
        if j % 2 == 1:
            for k in range(plane):
                if k % half == dy:
                    over_core[k].wait_recv()

        @pl.loop(0, groups // 2)
        def _(pair):
            rows = pl.ds(pl.multiple_of(pair * 16, 16), 16)
            block = gathered[
                q, pl.ds(pl.multiple_of(pair * 32, 16), 32), 0:quarter
            ].astype(F32)
            xs[q, rows, :] = jnp.concatenate([block[0:8], block[16:24]], axis=0).astype(BF16)
            dys[rows, :] = jnp.concatenate([block[8:16], block[24:32]], axis=0).astype(BF16)

        x = xs[q]
        dy_rows = dys[...]
        span = pl.ds(pl.multiple_of(q * quarter, LANES), quarter)
        logits[...] += contract_last(x, router_parts[:, span])
        for copy in weight_copies[j]:
            copy.wait()

        @pl.loop(0, ff_dev // tile)
        def _(n):
            cols = pl.ds(pl.multiple_of(n * tile, tile), tile)
            acc_gate[:, cols] += jnp.dot(x, gate[span, cols], preferred_element_type=F32)
            acc_up[:, cols] += jnp.dot(x, up[span, cols], preferred_element_type=F32)
            acc_down[:, cols] += contract_last(dy_rows, down[cols, span])

    lane = lax.broadcasted_iota(jnp.int32, (count, LANES), 1)
    meta = gathered[tensor, :, quarter : quarter + LANES].astype(F32)
    mask = jnp.concatenate([meta[16 * g : 16 * g + 8] for g in range(groups)], axis=0)
    parts = logits[...]
    summed = jnp.zeros((count, LANES), F32)
    for b in range(experts):
        column = jnp.sum(jnp.where(lane % 8 == b, parts, 0.0), axis=1, keepdims=True)
        summed = jnp.where(lane == b, column, summed)
    scores = jnp.where(mask > 0.5, jax.nn.sigmoid(summed), 0.0)
    totals = jnp.sum(scores, axis=1, keepdims=True)
    weights = scores / totals
    is_own = lane == expert
    weight_own[...] = jnp.broadcast_to(
        jnp.sum(jnp.where(is_own, weights, 0.0), axis=1, keepdims=True), (count, LANES)
    )

    @pl.loop(0, ff_dev // tile)
    def _(n):
        cols = pl.ds(pl.multiple_of(n * tile, tile), tile)
        pre_gate = acc_gate[:, cols]
        pre_up = acc_up[:, cols]
        plain = acc_down[:, cols]
        sig = jax.nn.sigmoid(pre_gate)
        act = pre_gate * sig
        hid = (act * pre_up).astype(BF16)
        hidden[:, cols] = hid
        grad_hidden = plain * weight_own[:, 0:1]
        grad_gate[:, cols] = (grad_hidden * pre_up * sig * (1.0 + pre_gate * (1.0 - sig))).astype(
            BF16
        )
        grad_up[:, cols] = (grad_hidden * act).astype(BF16)
        term = jnp.sum(hid.astype(F32) * plain, axis=1, keepdims=True)
        gw_own[0] += jnp.where(is_own, term, 0.0)

    gw_core = remote(gw_own.at[0], gw_own.at[3], sibling)

    for copy in sends[:gather_sends]:
        copy.wait_send()
    partial = gathered
    wide_tile = step_of(quarter, 512)

    def back(q, slot, added):
        h, gg, gu = hidden[...], grad_gate[...], grad_up[...]
        scale = weight_own[:, 0:1]

        @pl.loop(0, quarter // wide_tile)
        def _(n):
            cols = pl.ds(pl.multiple_of(n * wide_tile, LANES), wide_tile)
            span = pl.ds(pl.multiple_of(q * quarter + n * wide_tile, LANES), wide_tile)
            out = jnp.dot(h, down[:, span], preferred_element_type=F32) * scale
            grad = contract_last(gg, gate[span, :]) + contract_last(gu, up[span, :])
            for g in range(groups):
                both = jnp.concatenate([out[8 * g : 8 * g + 8], grad[8 * g : 8 * g + 8]], axis=0)
                if added is not None:
                    both = both + from_sibling[added, 16 * g : 16 * g + 16, cols].astype(F32)
                partial[slot, 16 * g : 16 * g + 16, cols] = both.astype(BF16)

    outer = list(range(1, half)) + [0]

    def target_at(dy, other):
        return ((row + dy) % half) * 2 + (1 - core if other else core)

    to_core = {}
    gw_over_plane = gw_over_expert = None
    for place, dy in enumerate(outer):
        back(target_at(dy, True), dy * 2 + 1, None)
        to_core[dy] = remote(partial.at[dy * 2 + 1, :, 0:quarter], from_sibling.at[dy], sibling)
        if place == 0:
            gw_core.wait_recv()
            gw_own[1] = gw_own[0] + gw_own[3]
            gw_over_plane = [
                remote(gw_own.at[1], gw_plane.at[k - 1], plane_peer(k)) for k in range(1, plane)
            ]
    for copy in gw_over_plane:
        copy.wait_recv()
    total = gw_own[1]
    for k in range(1, plane):
        total = total + gw_plane[k - 1]
    gw_own[2] = total
    gw_over_expert = [
        remote(gw_own.at[2], gw_expert.at[k - 1], expert_peer(k)) for k in range(1, experts)
    ]

    to_plane = {}
    for dy in outer:
        to_core[dy].wait_recv()
        back(target_at(dy, False), dy * 2, dy)
        for ds in range(sections):
            k = ds * half + dy
            if k:
                first = pl.multiple_of(((section + ds) % sections) * experts * 16, 16)
                to_plane[k] = remote(
                    partial.at[dy * 2, pl.ds(first, experts * 16), 0:quarter],
                    from_plane.at[k - 1],
                    plane_peer(k),
                )

    for copy in gw_over_expert:
        copy.wait_recv()
    grad_weight = gw_own[2]
    for k in range(1, experts):
        grad_weight = grad_weight + gw_expert[k - 1]
    cross = jnp.zeros((count, LANES), F32)
    for b in range(experts):
        is_b = lane == b
        other_score = jnp.sum(jnp.where(is_b, scores, 0.0), axis=1, keepdims=True)
        other_grad = jnp.sum(jnp.where(is_b, grad_weight, 0.0), axis=1, keepdims=True)
        cross = cross + jnp.where(is_b, 0.0, (grad_weight - other_grad) * other_score)
    grad_chosen = cross / (totals * totals) * scores * (1.0 - scores)
    grad_logits[...] = jnp.where(mask > 0.5, grad_chosen, 0.0)
    turned = grad_logits[...].T
    grad_router_ref[...] = jnp.dot(
        turned[0:8], xs[tensor].astype(F32), precision=precise, preferred_element_type=F32
    )[0:experts]
    own_rows = pl.ds(pl.multiple_of(group * 8, 8), 8)
    own_span = pl.ds(pl.multiple_of(tensor * quarter, LANES), quarter)
    through_router = jnp.dot(
        grad_logits[own_rows, 0:8],
        router_pad[:, own_span],
        precision=precise,
        preferred_element_type=F32,
    )

    for k in sorted(to_plane, key=lambda k: (-(k % half), k)):
        to_plane[k].wait_recv()
    own_section = pl.multiple_of(section * experts * 16, 16)

    @pl.loop(0, experts)
    def _(e):
        rows = pl.ds(pl.multiple_of(e * 16, 16), 16)
        home = pl.ds(pl.multiple_of(own_section + e * 16, 16), 16)
        value = partial[0, home, 0:quarter].astype(F32)
        for k in range(1, plane):
            value = value + from_plane[k - 1, rows, :].astype(F32)
        plane_sum[rows, :] = value.astype(BF16)

    back_home = []
    for k in range(1, experts):
        first = pl.multiple_of(((expert + k) % experts) * 16, 16)
        back_home.append(
            remote(plane_sum.at[pl.ds(first, 16), :], from_expert.at[k - 1], expert_peer(k))
        )
    value = plane_sum[pl.ds(pl.multiple_of(expert * 16, 16), 16), :].astype(F32)
    for k in range(1, experts):
        back_home[k - 1].wait_recv()
        value = value + from_expert[k - 1].astype(F32)
    moe_ref[...] = value[0:8].astype(BF16)
    grad_tokens_ref[...] = (value[8:16] + through_router).astype(BF16)

    for copy in sends[gather_sends:]:
        copy.wait_send()


def on_device(tokens, routes, router, gate_proj, up_proj, down_proj, grad_out):
    sections = lax.axis_size("section")
    experts = lax.axis_size("expert")
    tensors = lax.axis_size("tensor")
    quarter = tokens.shape[1]
    width = router.shape[0]
    ff_dev = gate_proj.shape[2]
    half = tensors // 2
    plane = sections * half
    groups = sections * experts
    count = groups * 8
    copies = 3 * (experts - 1) + 3 * (plane - 1) + plane + half + 1
    vmem = pl.BlockSpec(memory_space=pltpu.VMEM)
    hbm = pl.BlockSpec(memory_space=pl.ANY)
    moe_out, grad_tokens, grad_router = pl.pallas_call(
        functools.partial(layer_kernel, (sections, experts, tensors, quarter, ff_dev)),
        out_shape=(
            jax.ShapeDtypeStruct(tokens.shape, BF16),
            jax.ShapeDtypeStruct(tokens.shape, BF16),
            jax.ShapeDtypeStruct((experts, quarter), F32),
        ),
        in_specs=[vmem] * 4 + [hbm] * 3,
        out_specs=(vmem, vmem, vmem),
        scratch_shapes=[
            pltpu.VMEM((width, ff_dev), BF16),
            pltpu.VMEM((width, ff_dev), BF16),
            pltpu.VMEM((ff_dev, width), BF16),
            pltpu.VMEM((tensors, groups * 16, quarter + LANES), BF16),
            pltpu.VMEM((tensors, count, quarter), BF16),
            pltpu.VMEM((count, quarter), BF16),
            pltpu.VMEM((LANES, width), BF16),
            pltpu.VMEM((8, width), F32),
            pltpu.VMEM((count, LANES), F32),
            pltpu.VMEM((count, ff_dev), F32),
            pltpu.VMEM((count, ff_dev), F32),
            pltpu.VMEM((count, ff_dev), F32),
            pltpu.VMEM((count, ff_dev), BF16),
            pltpu.VMEM((count, ff_dev), BF16),
            pltpu.VMEM((count, ff_dev), BF16),
            pltpu.VMEM((count, LANES), F32),
            pltpu.VMEM((half, groups * 16, quarter), BF16),
            pltpu.VMEM((plane - 1, experts * 16, quarter), BF16),
            pltpu.VMEM((experts * 16, quarter), BF16),
            pltpu.VMEM((experts - 1, 16, quarter), BF16),
            pltpu.VMEM((4, count, LANES), F32),
            pltpu.VMEM((plane - 1, count, LANES), F32),
            pltpu.VMEM((experts - 1, count, LANES), F32),
            pltpu.VMEM((count, LANES), F32),
            pltpu.SemaphoreType.DMA((tensors, 3)),
            pltpu.SemaphoreType.DMA((copies,)),
            pltpu.SemaphoreType.DMA((copies,)),
        ],
        compiler_params=pltpu.CompilerParams(
            collective_id=0, has_side_effects=True, vmem_limit_bytes=58 * 1024 * 1024
        ),
    )(tokens, routes, router.T, grad_out, gate_proj[0], up_proj[0], down_proj[0])
    return (moe_out, grad_tokens, grad_router.T)


def solution(mesh):
    return jax.shard_map(
        on_device,
        mesh=mesh,
        in_specs=(
            P(("section", "expert"), "tensor"),
            P(("section", "expert"), None),
            P(),
            P("expert", None, ("section", "tensor")),
            P("expert", None, ("section", "tensor")),
            P("expert", ("section", "tensor"), None),
            P(("section", "expert"), "tensor"),
        ),
        out_specs=(
            P(("section", "expert"), "tensor"),
            P(("section", "expert"), "tensor"),
            P("tensor", None),
        ),
        check_vma=False,
    )
```

```python
import functools

import jax
import jax.numpy as jnp
from jax import lax
from jax.experimental import pallas as pl
from jax.experimental.pallas import tpu as pltpu
from jax.sharding import PartitionSpec as P

F32 = jnp.float32
BF16 = jnp.bfloat16
LANES = 128
precise = lax.Precision.HIGHEST


def contract_last(left, right):
    return lax.dot_general(left, right, (((1,), (1,)), ((), ())), preferred_element_type=F32)


def step_of(size, most):
    step = most
    while size % step:
        step //= 2
    return step


def layer_kernel(
    sizes,
    tokens_ref,
    routes_ref,
    router_ref,
    grad_out_ref,
    gate_hbm,
    up_hbm,
    down_hbm,
    moe_ref,
    grad_tokens_ref,
    grad_router_ref,
    gate,
    up,
    down,
    gathered,
    xs,
    dys,
    router_parts,
    router_pad,
    logits,
    acc_gate,
    acc_up,
    acc_down,
    hidden,
    grad_gate,
    grad_up,
    weight_own,
    from_sibling,
    from_plane,
    plane_sum,
    from_expert,
    gw_own,
    gw_plane,
    gw_expert,
    grad_logits,
    weight_sems,
    send_sems,
    recv_sems,
):
    sections, experts, tensors, quarter, ff_dev = sizes
    half = tensors // 2
    plane = sections * half
    groups = sections * experts
    count = groups * 8
    section = lax.axis_index("section")
    expert = lax.axis_index("expert")
    tensor = lax.axis_index("tensor")
    row = tensor // 2
    core = tensor % 2
    group = section * experts + expert
    here = {"section": section, "expert": expert, "tensor": tensor}

    def at(**moved):
        return {**here, **moved}

    def expert_peer(k):
        return at(expert=(expert + k) % experts)

    def plane_peer(k):
        return at(
            section=(section + k // half) % sections,
            tensor=((row + k % half) % half) * 2 + core,
        )

    sibling = at(tensor=row * 2 + 1 - core)
    used = [0]
    sends = []

    def remote(src, dst, peer):
        index = used[0]
        used[0] += 1
        copy = pltpu.make_async_remote_copy(
            src_ref=src,
            dst_ref=dst,
            send_sem=send_sems.at[index],
            recv_sem=recv_sems.at[index],
            device_id=peer,
            device_id_type=pl.DeviceIdType.MESH,
        )
        copy.start()
        sends.append(copy)
        return copy

    barrier = pltpu.get_barrier_semaphore()
    peers = (
        [expert_peer(k) for k in range(1, experts)]
        + [plane_peer(k) for k in range(1, plane)]
        + [sibling]
    )
    for peer in peers:
        pl.semaphore_signal(barrier, inc=1, device_id=peer, device_id_type=pl.DeviceIdType.MESH)

    def quarter_at(dy, other):
        return ((row + half - dy) % half) * 2 + (1 - core if other else core)

    order = [quarter_at(dy, other) for dy in range(half) for other in (False, True)]
    weight_copies = []
    for j, q in enumerate(order):
        span = pl.ds(pl.multiple_of(q * quarter, LANES), quarter)
        trio = [
            pltpu.make_async_copy(gate_hbm.at[span, :], gate.at[span, :], weight_sems.at[j, 0]),
            pltpu.make_async_copy(up_hbm.at[span, :], up.at[span, :], weight_sems.at[j, 1]),
            pltpu.make_async_copy(down_hbm.at[:, span], down.at[:, span], weight_sems.at[j, 2]),
        ]
        for copy in trio:
            copy.start()
        weight_copies.append(trio)

    lane8 = lax.broadcasted_iota(jnp.int32, (8, LANES), 1)
    routes = routes_ref[...].astype(F32)
    diagonal = lax.broadcasted_iota(jnp.int32, (8, 8), 0) == lax.broadcasted_iota(
        jnp.int32, (8, 8), 1
    )
    hot = jnp.zeros((8, LANES), F32)
    for k in range(routes.shape[0]):
        column = jnp.sum(jnp.where(diagonal, routes[k : k + 1, :], 0.0), axis=1, keepdims=True)
        hot = jnp.where(column == lane8.astype(F32), 1.0, hot)
    unit_rows = pl.ds(pl.multiple_of(group * 16, 16), 16)
    gathered[tensor, unit_rows, 0:quarter] = jnp.concatenate(
        [tokens_ref[...].astype(F32), grad_out_ref[...].astype(F32)], axis=0
    ).astype(BF16)
    gathered[tensor, unit_rows, quarter : quarter + LANES] = jnp.concatenate(
        [hot, jnp.zeros((8, LANES), F32)], axis=0
    ).astype(BF16)

    pl.semaphore_wait(barrier, len(peers))

    unit = gathered.at[tensor, unit_rows, :]
    over_expert = {k: remote(unit, unit, expert_peer(k)) for k in range(1, experts)}
    near = [k for k in range(1, plane) if k % half == 0]
    far = sorted([k for k in range(1, plane) if k % half], key=lambda k: (k % half, k // half))
    over_plane = {(k, 0): remote(unit, unit, plane_peer(k)) for k in near + far}

    router_pad[...] = jnp.zeros_like(router_pad)
    router_pad[0:experts, :] = router_ref[...]
    wide = router_pad[...]
    high = wide.astype(BF16).astype(F32)
    middle = (wide - high).astype(BF16).astype(F32)
    low = wide - high - middle
    router_parts[...] = jnp.zeros_like(router_parts)
    router_parts[0:32, :] = jnp.concatenate(
        [high, middle, low, jnp.zeros_like(low)], axis=0
    ).astype(BF16)
    logits[...] = jnp.zeros_like(logits)
    acc_gate[...] = jnp.zeros_like(acc_gate)
    acc_up[...] = jnp.zeros_like(acc_up)
    acc_down[...] = jnp.zeros_like(acc_down)
    gw_own[...] = jnp.zeros_like(gw_own)

    for j in sorted(range(1, experts), key=lambda j: (min(j, experts - j), j)):
        over_expert[j].wait_recv()
        first = (section * experts + (expert + experts - j) % experts) * 16
        landed = gathered.at[tensor, pl.ds(pl.multiple_of(first, 16), 16), :]
        for k in near + far:
            over_plane[k, j] = remote(landed, landed, plane_peer(k))

    def chunk_of(k):
        from_section = (section + sections - k // half) % sections
        from_tensor = quarter_at(k % half, False)
        rows = pl.ds(pl.multiple_of(from_section * experts * 16, 16), experts * 16)
        return gathered.at[from_tensor, rows, :]

    over_core = {0: remote(chunk_of(0), chunk_of(0), sibling)}

    def hand_on(k):
        for j in range(experts):
            over_plane[k, j].wait_recv()
        over_core[k] = remote(chunk_of(k), chunk_of(k), sibling)

    for k in near:
        hand_on(k)

    tile = step_of(ff_dev, 256)
    for j, q in enumerate(order):
        dy = j // 2
        if j == 1:
            for k in far:
                hand_on(k)
        if j % 2 == 1:
            for k in range(plane):
                if k % half == dy:
                    over_core[k].wait_recv()

        @pl.loop(0, groups // 2)
        def _(pair):
            rows = pl.ds(pl.multiple_of(pair * 16, 16), 16)
            block = gathered[
                q, pl.ds(pl.multiple_of(pair * 32, 16), 32), 0:quarter
            ].astype(F32)
            xs[q, rows, :] = jnp.concatenate([block[0:8], block[16:24]], axis=0).astype(BF16)
            dys[rows, :] = jnp.concatenate([block[8:16], block[24:32]], axis=0).astype(BF16)

        x = xs[q]
        dy_rows = dys[...]
        span = pl.ds(pl.multiple_of(q * quarter, LANES), quarter)
        logits[...] += contract_last(x, router_parts[:, span])
        for copy in weight_copies[j]:
            copy.wait()

        @pl.loop(0, ff_dev // tile)
        def _(n):
            cols = pl.ds(pl.multiple_of(n * tile, tile), tile)
            acc_gate[:, cols] += jnp.dot(x, gate[span, cols], preferred_element_type=F32)
            acc_up[:, cols] += jnp.dot(x, up[span, cols], preferred_element_type=F32)
            acc_down[:, cols] += contract_last(dy_rows, down[cols, span])

    gather_sends = len(sends)

    lane = lax.broadcasted_iota(jnp.int32, (count, LANES), 1)
    meta = gathered[tensor, :, quarter : quarter + LANES].astype(F32)
    mask = jnp.concatenate([meta[16 * g : 16 * g + 8] for g in range(groups)], axis=0)
    parts = logits[...]
    summed = jnp.zeros((count, LANES), F32)
    for b in range(experts):
        column = jnp.sum(jnp.where(lane % 8 == b, parts, 0.0), axis=1, keepdims=True)
        summed = jnp.where(lane == b, column, summed)
    scores = jnp.where(mask > 0.5, jax.nn.sigmoid(summed), 0.0)
    totals = jnp.sum(scores, axis=1, keepdims=True)
    weights = scores / totals
    is_own = lane == expert
    weight_own[...] = jnp.broadcast_to(
        jnp.sum(jnp.where(is_own, weights, 0.0), axis=1, keepdims=True), (count, LANES)
    )

    @pl.loop(0, ff_dev // tile)
    def _(n):
        cols = pl.ds(pl.multiple_of(n * tile, tile), tile)
        pre_gate = acc_gate[:, cols]
        pre_up = acc_up[:, cols]
        plain = acc_down[:, cols]
        sig = jax.nn.sigmoid(pre_gate)
        act = pre_gate * sig
        hid = (act * pre_up).astype(BF16)
        hidden[:, cols] = hid
        grad_hidden = plain * weight_own[:, 0:1]
        grad_gate[:, cols] = (grad_hidden * pre_up * sig * (1.0 + pre_gate * (1.0 - sig))).astype(
            BF16
        )
        grad_up[:, cols] = (grad_hidden * act).astype(BF16)
        term = jnp.sum(hid.astype(F32) * plain, axis=1, keepdims=True)
        gw_own[0] += jnp.where(is_own, term, 0.0)

    gw_core = remote(gw_own.at[0], gw_own.at[3], sibling)

    for copy in sends[:gather_sends]:
        copy.wait_send()
    partial = gathered
    wide_tile = step_of(quarter, 512)

    tiles = quarter // wide_tile

    def back_tile(q, slot, added, n):
        cols = pl.ds(pl.multiple_of(n * wide_tile, LANES), wide_tile)
        span = pl.ds(pl.multiple_of(q * quarter + n * wide_tile, LANES), wide_tile)
        out = jnp.dot(hidden[...], down[:, span], preferred_element_type=F32)
        out = out * weight_own[:, 0:1]
        grad = contract_last(grad_gate[...], gate[span, :])
        grad = grad + contract_last(grad_up[...], up[span, :])
        for g in range(groups):
            both = jnp.concatenate([out[8 * g : 8 * g + 8], grad[8 * g : 8 * g + 8]], axis=0)
            if added is not None:
                both = both + from_sibling[added, 16 * g : 16 * g + 16, cols].astype(F32)
            partial[slot, 16 * g : 16 * g + 16, cols] = both.astype(BF16)

    def back(q, slot, added):
        @pl.loop(0, tiles)
        def _(n):
            back_tile(q, slot, added, n)

    outer = list(range(1, half)) + [0]

    def target_at(dy, other):
        return ((row + dy) % half) * 2 + (1 - core if other else core)

    to_core = {}
    gw_over_plane = gw_over_expert = None
    for place, dy in enumerate(outer):
        back(target_at(dy, True), dy * 2 + 1, None)
        to_core[dy] = remote(partial.at[dy * 2 + 1, :, 0:quarter], from_sibling.at[dy], sibling)
        if place == 0:
            gw_core.wait_recv()
            gw_own[1] = gw_own[0] + gw_own[3]
            gw_over_plane = [
                remote(gw_own.at[1], gw_plane.at[k - 1], plane_peer(k)) for k in range(1, plane)
            ]
    for copy in gw_over_plane:
        copy.wait_recv()
    total = gw_own[1]
    for k in range(1, plane):
        total = total + gw_plane[k - 1]
    gw_own[2] = total
    gw_over_expert = [
        remote(gw_own.at[2], gw_expert.at[k - 1], expert_peer(k)) for k in range(1, experts)
    ]

    def section_rows(ds):
        first = pl.multiple_of(((section + ds) % sections) * experts * 16, 16)
        return pl.ds(first, experts * 16)

    to_plane = {}
    for dy in outer[:-1]:
        to_core[dy].wait_recv()
        back(target_at(dy, False), dy * 2, dy)
        for ds in range(sections):
            k = ds * half + dy
            to_plane[k] = remote(
                partial.at[dy * 2, section_rows(ds), 0:quarter],
                from_plane.at[k - 1],
                plane_peer(k),
            )

    to_core[0].wait_recv()
    spans = [slice(n * wide_tile, (n + 1) * wide_tile) for n in range(tiles)]
    for n, cols in enumerate(spans):
        back_tile(target_at(0, False), 0, 0, n)
        for ds in range(1, sections):
            k = ds * half
            to_plane[k, n] = remote(
                partial.at[0, section_rows(ds), cols],
                from_plane.at[k - 1, :, cols],
                plane_peer(k),
            )

    for k in far:
        to_plane[k].wait_recv()
    own_section = pl.multiple_of(section * experts * 16, 16)
    back_home = {}
    for n, cols in enumerate(spans):
        for k in near:
            to_plane[k, n].wait_recv()

        @pl.loop(0, experts)
        def _(e):
            rows = pl.ds(pl.multiple_of(e * 16, 16), 16)
            home = pl.ds(pl.multiple_of(own_section + e * 16, 16), 16)
            value = partial[0, home, cols].astype(F32)
            for k in range(1, plane):
                value = value + from_plane[k - 1, rows, cols].astype(F32)
            plane_sum[rows, cols] = value.astype(BF16)

        for k in range(1, experts):
            first = pl.multiple_of(((expert + k) % experts) * 16, 16)
            back_home[k, n] = remote(
                plane_sum.at[pl.ds(first, 16), cols],
                from_expert.at[k - 1, :, cols],
                expert_peer(k),
            )

    for copy in gw_over_expert:
        copy.wait_recv()
    grad_weight = gw_own[2]
    for k in range(1, experts):
        grad_weight = grad_weight + gw_expert[k - 1]
    cross = jnp.zeros((count, LANES), F32)
    for b in range(experts):
        is_b = lane == b
        other_score = jnp.sum(jnp.where(is_b, scores, 0.0), axis=1, keepdims=True)
        other_grad = jnp.sum(jnp.where(is_b, grad_weight, 0.0), axis=1, keepdims=True)
        cross = cross + jnp.where(is_b, 0.0, (grad_weight - other_grad) * other_score)
    grad_chosen = cross / (totals * totals) * scores * (1.0 - scores)
    grad_logits[...] = jnp.where(mask > 0.5, grad_chosen, 0.0)
    turned = grad_logits[...].T
    grad_router_ref[...] = jnp.dot(
        turned[0:8], xs[tensor].astype(F32), precision=precise, preferred_element_type=F32
    )[0:experts]
    own_rows = pl.ds(pl.multiple_of(group * 8, 8), 8)
    own_span = pl.ds(pl.multiple_of(tensor * quarter, LANES), quarter)
    through_router = jnp.dot(
        grad_logits[own_rows, 0:8],
        router_pad[:, own_span],
        precision=precise,
        preferred_element_type=F32,
    )

    value = plane_sum[pl.ds(pl.multiple_of(expert * 16, 16), 16), :].astype(F32)
    for copy in back_home.values():
        copy.wait_recv()
    for k in range(1, experts):
        value = value + from_expert[k - 1].astype(F32)
    moe_ref[...] = value[0:8].astype(BF16)
    grad_tokens_ref[...] = (value[8:16] + through_router).astype(BF16)

    for copy in sends[gather_sends:]:
        copy.wait_send()


def hand_over_kernel(moe_ref, tokens_ref, router_ref, moe_out, tokens_out, router_out):
    moe_out[...] = moe_ref[...]
    tokens_out[...] = tokens_ref[...]
    router_out[...] = router_ref[...]


def on_device(tokens, routes, router, gate_proj, up_proj, down_proj, grad_out):
    sections = lax.axis_size("section")
    experts = lax.axis_size("expert")
    tensors = lax.axis_size("tensor")
    quarter = tokens.shape[1]
    width = router.shape[0]
    ff_dev = gate_proj.shape[2]
    half = tensors // 2
    plane = sections * half
    groups = sections * experts
    count = groups * 8
    tiles = quarter // step_of(quarter, 512)
    near = sections - 1
    copies = (2 + tiles) * (experts - 1) + (1 + experts) * (plane - 1) + plane + half + 1
    copies += plane - 1 - near + tiles * near
    vmem = pl.BlockSpec(memory_space=pltpu.VMEM)
    hbm = pl.BlockSpec(memory_space=pl.ANY)
    moe_out, grad_tokens, grad_router = pl.pallas_call(
        functools.partial(layer_kernel, (sections, experts, tensors, quarter, ff_dev)),
        out_shape=(
            jax.ShapeDtypeStruct(tokens.shape, BF16),
            jax.ShapeDtypeStruct(tokens.shape, BF16),
            jax.ShapeDtypeStruct((experts, quarter), F32),
        ),
        in_specs=[vmem] * 4 + [hbm] * 3,
        out_specs=(vmem, vmem, vmem),
        scratch_shapes=[
            pltpu.VMEM((width, ff_dev), BF16),
            pltpu.VMEM((width, ff_dev), BF16),
            pltpu.VMEM((ff_dev, width), BF16),
            pltpu.VMEM((tensors, groups * 16, quarter + LANES), BF16),
            pltpu.VMEM((tensors, count, quarter), BF16),
            pltpu.VMEM((count, quarter), BF16),
            pltpu.VMEM((LANES, width), BF16),
            pltpu.VMEM((8, width), F32),
            pltpu.VMEM((count, LANES), F32),
            pltpu.VMEM((count, ff_dev), F32),
            pltpu.VMEM((count, ff_dev), F32),
            pltpu.VMEM((count, ff_dev), F32),
            pltpu.VMEM((count, ff_dev), BF16),
            pltpu.VMEM((count, ff_dev), BF16),
            pltpu.VMEM((count, ff_dev), BF16),
            pltpu.VMEM((count, LANES), F32),
            pltpu.VMEM((half, groups * 16, quarter), BF16),
            pltpu.VMEM((plane - 1, experts * 16, quarter), BF16),
            pltpu.VMEM((experts * 16, quarter), BF16),
            pltpu.VMEM((experts - 1, 16, quarter), BF16),
            pltpu.VMEM((4, count, LANES), F32),
            pltpu.VMEM((plane - 1, count, LANES), F32),
            pltpu.VMEM((experts - 1, count, LANES), F32),
            pltpu.VMEM((count, LANES), F32),
            pltpu.SemaphoreType.DMA((tensors, 3)),
            pltpu.SemaphoreType.DMA((copies,)),
            pltpu.SemaphoreType.DMA((copies,)),
        ],
        compiler_params=pltpu.CompilerParams(
            collective_id=0, has_side_effects=True, vmem_limit_bytes=58 * 1024 * 1024
        ),
    )(tokens, routes.T, router.T, grad_out, gate_proj[0], up_proj[0], down_proj[0])
    moe_out, grad_tokens, grad_router = pl.pallas_call(
        hand_over_kernel,
        out_shape=tuple(
            jax.ShapeDtypeStruct(part.shape, part.dtype)
            for part in (moe_out, grad_tokens, grad_router)
        ),
        in_specs=[vmem] * 3,
        out_specs=(vmem, vmem, vmem),
    )(moe_out, grad_tokens, grad_router)
    return (moe_out, grad_tokens, grad_router.T)


def solution(mesh):
    return jax.shard_map(
        on_device,
        mesh=mesh,
        in_specs=(
            P(("section", "expert"), "tensor"),
            P(("section", "expert"), None),
            P(),
            P("expert", None, ("section", "tensor")),
            P("expert", None, ("section", "tensor")),
            P("expert", ("section", "tensor"), None),
            P(("section", "expert"), "tensor"),
        ),
        out_specs=(
            P(("section", "expert"), "tensor"),
            P(("section", "expert"), "tensor"),
            P("tensor", None),
        ),
        check_vma=False,
    )
```

```python
import functools

import jax
import jax.numpy as jnp
from jax import lax
from jax.experimental import pallas as pl
from jax.experimental.pallas import tpu as pltpu
from jax.sharding import PartitionSpec as P

F32 = jnp.float32
BF16 = jnp.bfloat16
LANES = 128
precise = lax.Precision.HIGHEST


def contract_last(left, right):
    return lax.dot_general(left, right, (((1,), (1,)), ((), ())), preferred_element_type=F32)


def step_of(size, most):
    step = most
    while size % step:
        step //= 2
    return step


def layer_kernel(
    sizes,
    tokens_ref,
    routes_ref,
    router_ref,
    grad_out_ref,
    gate_hbm,
    up_hbm,
    down_hbm,
    moe_ref,
    grad_tokens_ref,
    grad_router_ref,
    gate,
    up,
    down,
    gathered,
    xs,
    dys,
    router_parts,
    router_pad,
    logits,
    acc_gate,
    acc_up,
    acc_down,
    hidden,
    grad_gate,
    grad_up,
    weight_own,
    from_sibling,
    from_plane,
    plane_sum,
    from_expert,
    gw_own,
    gw_plane,
    gw_expert,
    grad_logits,
    weight_sems,
    send_sems,
    recv_sems,
):
    sections, experts, tensors, quarter, ff_dev = sizes
    half = tensors // 2
    plane = sections * half
    groups = sections * experts
    count = groups * 8
    section = lax.axis_index("section")
    expert = lax.axis_index("expert")
    tensor = lax.axis_index("tensor")
    row = tensor // 2
    core = tensor % 2
    group = section * experts + expert
    here = {"section": section, "expert": expert, "tensor": tensor}

    def at(**moved):
        return {**here, **moved}

    def expert_peer(k):
        return at(expert=(expert + k) % experts)

    def plane_peer(k):
        return at(
            section=(section + k // half) % sections,
            tensor=((row + k % half) % half) * 2 + core,
        )

    sibling = at(tensor=row * 2 + 1 - core)
    used = [0]
    sends = []

    def remote(src, dst, peer):
        index = used[0]
        used[0] += 1
        copy = pltpu.make_async_remote_copy(
            src_ref=src,
            dst_ref=dst,
            send_sem=send_sems.at[index],
            recv_sem=recv_sems.at[index],
            device_id=peer,
            device_id_type=pl.DeviceIdType.MESH,
        )
        copy.start()
        sends.append(copy)
        return copy

    barrier = pltpu.get_barrier_semaphore()
    peers = (
        [expert_peer(k) for k in range(1, experts)]
        + [plane_peer(k) for k in range(1, plane)]
        + [sibling]
    )
    for peer in peers:
        pl.semaphore_signal(barrier, inc=1, device_id=peer, device_id_type=pl.DeviceIdType.MESH)

    def quarter_at(dy, other):
        return ((row + half - dy) % half) * 2 + (1 - core if other else core)

    order = [quarter_at(dy, other) for dy in range(half) for other in (False, True)]
    weight_copies = []
    for j, q in enumerate(order):
        span = pl.ds(pl.multiple_of(q * quarter, LANES), quarter)
        trio = [
            pltpu.make_async_copy(gate_hbm.at[span, :], gate.at[span, :], weight_sems.at[j, 0]),
            pltpu.make_async_copy(up_hbm.at[span, :], up.at[span, :], weight_sems.at[j, 1]),
            pltpu.make_async_copy(down_hbm.at[:, span], down.at[:, span], weight_sems.at[j, 2]),
        ]
        for copy in trio:
            copy.start()
        weight_copies.append(trio)

    lane8 = lax.broadcasted_iota(jnp.int32, (8, LANES), 1)
    routes = routes_ref[...].astype(F32)
    diagonal = lax.broadcasted_iota(jnp.int32, (8, 8), 0) == lax.broadcasted_iota(
        jnp.int32, (8, 8), 1
    )
    hot = jnp.zeros((8, LANES), F32)
    for k in range(routes.shape[0]):
        column = jnp.sum(jnp.where(diagonal, routes[k : k + 1, :], 0.0), axis=1, keepdims=True)
        hot = jnp.where(column == lane8.astype(F32), 1.0, hot)
    unit_rows = pl.ds(pl.multiple_of(group * 16, 16), 16)
    gathered[tensor, unit_rows, 0:quarter] = jnp.concatenate(
        [tokens_ref[...].astype(F32), grad_out_ref[...].astype(F32)], axis=0
    ).astype(BF16)
    gathered[tensor, unit_rows, quarter : quarter + LANES] = jnp.concatenate(
        [hot, jnp.zeros((8, LANES), F32)], axis=0
    ).astype(BF16)

    pl.semaphore_wait(barrier, len(peers))

    unit = gathered.at[tensor, unit_rows, :]
    over_expert = {k: remote(unit, unit, expert_peer(k)) for k in range(1, experts)}
    near = [k for k in range(1, plane) if k % half == 0]
    far = sorted([k for k in range(1, plane) if k % half], key=lambda k: (k % half, k // half))
    over_plane = {(k, 0): remote(unit, unit, plane_peer(k)) for k in near + far}

    router_pad[...] = jnp.zeros_like(router_pad)
    router_pad[0:experts, :] = router_ref[...]
    wide = router_pad[...]
    high = wide.astype(BF16).astype(F32)
    middle = (wide - high).astype(BF16).astype(F32)
    low = wide - high - middle
    router_parts[...] = jnp.zeros_like(router_parts)
    router_parts[0:32, :] = jnp.concatenate(
        [high, middle, low, jnp.zeros_like(low)], axis=0
    ).astype(BF16)
    logits[...] = jnp.zeros_like(logits)
    acc_gate[...] = jnp.zeros_like(acc_gate)
    acc_up[...] = jnp.zeros_like(acc_up)
    acc_down[...] = jnp.zeros_like(acc_down)
    gw_own[...] = jnp.zeros_like(gw_own)

    for j in sorted(range(1, experts), key=lambda j: (min(j, experts - j), j)):
        over_expert[j].wait_recv()
        first = (section * experts + (expert + experts - j) % experts) * 16
        landed = gathered.at[tensor, pl.ds(pl.multiple_of(first, 16), 16), :]
        for k in near + far:
            over_plane[k, j] = remote(landed, landed, plane_peer(k))

    def chunk_of(k):
        from_section = (section + sections - k // half) % sections
        from_tensor = quarter_at(k % half, False)
        rows = pl.ds(pl.multiple_of(from_section * experts * 16, 16), experts * 16)
        return gathered.at[from_tensor, rows, :]

    over_core = {0: remote(chunk_of(0), chunk_of(0), sibling)}

    def hand_on(k):
        for j in range(experts):
            over_plane[k, j].wait_recv()
        over_core[k] = remote(chunk_of(k), chunk_of(k), sibling)

    for k in near:
        hand_on(k)

    tile = step_of(ff_dev, 512)
    for j, q in enumerate(order):
        dy = j // 2
        if j == 1:
            for k in far:
                hand_on(k)
        if j % 2 == 1:
            for k in range(plane):
                if k % half == dy:
                    over_core[k].wait_recv()

        @pl.loop(0, groups // 2)
        def _(pair):
            rows = pl.ds(pl.multiple_of(pair * 16, 16), 16)
            block = gathered[
                q, pl.ds(pl.multiple_of(pair * 32, 16), 32), 0:quarter
            ].astype(F32)
            xs[q, rows, :] = jnp.concatenate([block[0:8], block[16:24]], axis=0).astype(BF16)
            dys[rows, :] = jnp.concatenate([block[8:16], block[24:32]], axis=0).astype(BF16)

        x = xs[q]
        dy_rows = dys[...]
        span = pl.ds(pl.multiple_of(q * quarter, LANES), quarter)
        logits[...] += contract_last(x, router_parts[:, span])
        for copy in weight_copies[j]:
            copy.wait()

        @pl.loop(0, ff_dev // tile)
        def _(n):
            cols = pl.ds(pl.multiple_of(n * tile, tile), tile)
            acc_gate[:, cols] += jnp.dot(x, gate[span, cols], preferred_element_type=F32)
            acc_up[:, cols] += jnp.dot(x, up[span, cols], preferred_element_type=F32)
            acc_down[:, cols] += contract_last(dy_rows, down[cols, span])

    gather_sends = len(sends)

    lane = lax.broadcasted_iota(jnp.int32, (count, LANES), 1)
    meta = gathered[tensor, :, quarter : quarter + LANES].astype(F32)
    mask = jnp.concatenate([meta[16 * g : 16 * g + 8] for g in range(groups)], axis=0)
    parts = logits[...]
    summed = jnp.zeros((count, LANES), F32)
    for b in range(experts):
        column = jnp.sum(jnp.where(lane % 8 == b, parts, 0.0), axis=1, keepdims=True)
        summed = jnp.where(lane == b, column, summed)
    scores = jnp.where(mask > 0.5, jax.nn.sigmoid(summed), 0.0)
    totals = jnp.sum(scores, axis=1, keepdims=True)
    weights = scores / totals
    is_own = lane == expert
    weight_own[...] = jnp.broadcast_to(
        jnp.sum(jnp.where(is_own, weights, 0.0), axis=1, keepdims=True), (count, LANES)
    )

    tile = step_of(ff_dev, 256)

    @pl.loop(0, ff_dev // tile)
    def _(n):
        cols = pl.ds(pl.multiple_of(n * tile, tile), tile)
        pre_gate = acc_gate[:, cols]
        pre_up = acc_up[:, cols]
        plain = acc_down[:, cols]
        sig = jax.nn.sigmoid(pre_gate)
        act = pre_gate * sig
        hid = (act * pre_up).astype(BF16)
        hidden[:, cols] = hid
        grad_hidden = plain * weight_own[:, 0:1]
        grad_gate[:, cols] = (grad_hidden * pre_up * sig * (1.0 + pre_gate * (1.0 - sig))).astype(
            BF16
        )
        grad_up[:, cols] = (grad_hidden * act).astype(BF16)
        term = jnp.sum(hid.astype(F32) * plain, axis=1, keepdims=True)
        gw_own[0] += jnp.where(is_own, term, 0.0)

    gw_core = remote(gw_own.at[0], gw_own.at[3], sibling)

    for copy in sends[:gather_sends]:
        copy.wait_send()
    partial = gathered
    wide_tile = step_of(quarter, 512)

    tiles = quarter // wide_tile

    def back_tile(q, slot, added, n):
        cols = pl.ds(pl.multiple_of(n * wide_tile, LANES), wide_tile)
        span = pl.ds(pl.multiple_of(q * quarter + n * wide_tile, LANES), wide_tile)
        out = jnp.dot(hidden[...], down[:, span], preferred_element_type=F32)
        out = out * weight_own[:, 0:1]
        grad = contract_last(grad_gate[...], gate[span, :])
        grad = grad + contract_last(grad_up[...], up[span, :])
        for g in range(groups):
            both = jnp.concatenate([out[8 * g : 8 * g + 8], grad[8 * g : 8 * g + 8]], axis=0)
            if added is not None:
                both = both + from_sibling[added, 16 * g : 16 * g + 16, cols].astype(F32)
            partial[slot, 16 * g : 16 * g + 16, cols] = both.astype(BF16)

    def back(q, slot, added):
        @pl.loop(0, tiles)
        def _(n):
            back_tile(q, slot, added, n)

    outer = list(range(1, half)) + [0]

    def target_at(dy, other):
        return ((row + dy) % half) * 2 + (1 - core if other else core)

    to_core = {}
    gw_over_plane = gw_over_expert = None
    for place, dy in enumerate(outer):
        back(target_at(dy, True), dy * 2 + 1, None)
        to_core[dy] = remote(partial.at[dy * 2 + 1, :, 0:quarter], from_sibling.at[dy], sibling)
        if place == 0:
            gw_core.wait_recv()
            gw_own[1] = gw_own[0] + gw_own[3]
            gw_over_plane = [
                remote(gw_own.at[1], gw_plane.at[k - 1], plane_peer(k)) for k in range(1, plane)
            ]
    for copy in gw_over_plane:
        copy.wait_recv()
    total = gw_own[1]
    for k in range(1, plane):
        total = total + gw_plane[k - 1]
    gw_own[2] = total
    gw_over_expert = [
        remote(gw_own.at[2], gw_expert.at[k - 1], expert_peer(k)) for k in range(1, experts)
    ]

    def section_rows(ds):
        first = pl.multiple_of(((section + ds) % sections) * experts * 16, 16)
        return pl.ds(first, experts * 16)

    own_section = pl.multiple_of(section * experts * 16, 16)
    spans = [slice(n * wide_tile, (n + 1) * wide_tile) for n in range(tiles)]
    to_plane = {}
    back_home = {}

    def finish(n):
        cols = spans[n]
        for k in range(1, plane):
            to_plane[k, n].wait_recv()

        @pl.loop(0, experts)
        def _(e):
            rows = pl.ds(pl.multiple_of(e * 16, 16), 16)
            home = pl.ds(pl.multiple_of(own_section + e * 16, 16), 16)
            value = partial[0, home, cols].astype(F32)
            for k in range(1, plane):
                value = value + from_plane[k - 1, rows, cols].astype(F32)
            plane_sum[rows, cols] = value.astype(BF16)

        for k in range(1, experts):
            first = pl.multiple_of(((expert + k) % experts) * 16, 16)
            back_home[k, n] = remote(
                plane_sum.at[pl.ds(first, 16), cols],
                from_expert.at[k - 1, :, cols],
                expert_peer(k),
            )

    for n, cols in enumerate(spans):
        for dy in outer:
            if n == 0:
                to_core[dy].wait_recv()
            back_tile(target_at(dy, False), dy * 2, dy, n)
            for ds in range(sections):
                k = ds * half + dy
                if k:
                    to_plane[k, n] = remote(
                        partial.at[dy * 2, section_rows(ds), cols],
                        from_plane.at[k - 1, :, cols],
                        plane_peer(k),
                    )
        if n:
            finish(n - 1)
    finish(tiles - 1)

    for copy in gw_over_expert:
        copy.wait_recv()
    grad_weight = gw_own[2]
    for k in range(1, experts):
        grad_weight = grad_weight + gw_expert[k - 1]
    cross = jnp.zeros((count, LANES), F32)
    for b in range(experts):
        is_b = lane == b
        other_score = jnp.sum(jnp.where(is_b, scores, 0.0), axis=1, keepdims=True)
        other_grad = jnp.sum(jnp.where(is_b, grad_weight, 0.0), axis=1, keepdims=True)
        cross = cross + jnp.where(is_b, 0.0, (grad_weight - other_grad) * other_score)
    grad_chosen = cross / (totals * totals) * scores * (1.0 - scores)
    grad_logits[...] = jnp.where(mask > 0.5, grad_chosen, 0.0)
    turned = grad_logits[...].T
    grad_router_ref[...] = jnp.dot(
        turned[0:8], xs[tensor].astype(F32), precision=precise, preferred_element_type=F32
    )[0:experts]
    own_rows = pl.ds(pl.multiple_of(group * 8, 8), 8)
    own_span = pl.ds(pl.multiple_of(tensor * quarter, LANES), quarter)
    through_router = jnp.dot(
        grad_logits[own_rows, 0:8],
        router_pad[:, own_span],
        precision=precise,
        preferred_element_type=F32,
    )

    value = plane_sum[pl.ds(pl.multiple_of(expert * 16, 16), 16), :].astype(F32)
    for copy in back_home.values():
        copy.wait_recv()
    for k in range(1, experts):
        value = value + from_expert[k - 1].astype(F32)
    moe_ref[...] = value[0:8].astype(BF16)
    grad_tokens_ref[...] = (value[8:16] + through_router).astype(BF16)

    for copy in sends[gather_sends:]:
        copy.wait_send()


def hand_over_kernel(moe_ref, tokens_ref, router_ref, moe_out, tokens_out, router_out):
    moe_out[...] = moe_ref[...]
    tokens_out[...] = tokens_ref[...]
    router_out[...] = router_ref[...]


def on_device(tokens, routes, router, gate_proj, up_proj, down_proj, grad_out):
    sections = lax.axis_size("section")
    experts = lax.axis_size("expert")
    tensors = lax.axis_size("tensor")
    quarter = tokens.shape[1]
    width = router.shape[0]
    ff_dev = gate_proj.shape[2]
    half = tensors // 2
    plane = sections * half
    groups = sections * experts
    count = groups * 8
    tiles = quarter // step_of(quarter, 512)
    copies = (2 + tiles) * (experts - 1) + (1 + experts + tiles) * (plane - 1) + plane + half + 1
    vmem = pl.BlockSpec(memory_space=pltpu.VMEM)
    hbm = pl.BlockSpec(memory_space=pl.ANY)
    moe_out, grad_tokens, grad_router = pl.pallas_call(
        functools.partial(layer_kernel, (sections, experts, tensors, quarter, ff_dev)),
        out_shape=(
            jax.ShapeDtypeStruct(tokens.shape, BF16),
            jax.ShapeDtypeStruct(tokens.shape, BF16),
            jax.ShapeDtypeStruct((experts, quarter), F32),
        ),
        in_specs=[vmem] * 4 + [hbm] * 3,
        out_specs=(vmem, vmem, vmem),
        scratch_shapes=[
            pltpu.VMEM((width, ff_dev), BF16),
            pltpu.VMEM((width, ff_dev), BF16),
            pltpu.VMEM((ff_dev, width), BF16),
            pltpu.VMEM((tensors, groups * 16, quarter + LANES), BF16),
            pltpu.VMEM((tensors, count, quarter), BF16),
            pltpu.VMEM((count, quarter), BF16),
            pltpu.VMEM((LANES, width), BF16),
            pltpu.VMEM((8, width), F32),
            pltpu.VMEM((count, LANES), F32),
            pltpu.VMEM((count, ff_dev), F32),
            pltpu.VMEM((count, ff_dev), F32),
            pltpu.VMEM((count, ff_dev), F32),
            pltpu.VMEM((count, ff_dev), BF16),
            pltpu.VMEM((count, ff_dev), BF16),
            pltpu.VMEM((count, ff_dev), BF16),
            pltpu.VMEM((count, LANES), F32),
            pltpu.VMEM((half, groups * 16, quarter), BF16),
            pltpu.VMEM((plane - 1, experts * 16, quarter), BF16),
            pltpu.VMEM((experts * 16, quarter), BF16),
            pltpu.VMEM((experts - 1, 16, quarter), BF16),
            pltpu.VMEM((4, count, LANES), F32),
            pltpu.VMEM((plane - 1, count, LANES), F32),
            pltpu.VMEM((experts - 1, count, LANES), F32),
            pltpu.VMEM((count, LANES), F32),
            pltpu.SemaphoreType.DMA((tensors, 3)),
            pltpu.SemaphoreType.DMA((copies,)),
            pltpu.SemaphoreType.DMA((copies,)),
        ],
        compiler_params=pltpu.CompilerParams(
            collective_id=0, has_side_effects=True, vmem_limit_bytes=58 * 1024 * 1024
        ),
    )(tokens, routes.T, router.T, grad_out, gate_proj[0], up_proj[0], down_proj[0])
    moe_out, grad_tokens, grad_router = pl.pallas_call(
        hand_over_kernel,
        out_shape=tuple(
            jax.ShapeDtypeStruct(part.shape, part.dtype)
            for part in (moe_out, grad_tokens, grad_router)
        ),
        in_specs=[vmem] * 3,
        out_specs=(vmem, vmem, vmem),
    )(moe_out, grad_tokens, grad_router)
    return (moe_out, grad_tokens, grad_router.T)


def solution(mesh):
    return jax.shard_map(
        on_device,
        mesh=mesh,
        in_specs=(
            P(("section", "expert"), "tensor"),
            P(("section", "expert"), None),
            P(),
            P("expert", None, ("section", "tensor")),
            P("expert", None, ("section", "tensor")),
            P("expert", ("section", "tensor"), None),
            P(("section", "expert"), "tensor"),
        ),
        out_specs=(
            P(("section", "expert"), "tensor"),
            P(("section", "expert"), "tensor"),
            P("tensor", None),
        ),
        check_vma=False,
    )
```
